32 devices in a mesh: leaf: 32 (over z, y, x, core).
Axes of the slice: x: 2, y: 2, z: 4, core: 2. Of those that a mesh axis runs over, the one named last changes fastest.
Arguments:
- right_sides: bfloat16 [64, 32768], P(None, 'leaf'), may hold values from -6 to 6
- leaf_inverse: bfloat16 [32768, 1024], P('leaf'), may hold values from -0.1875 to 0.1875
- leaf_basis: bfloat16 [32768, 256], P('leaf'), may hold values from -0.1875 to 0.1875
- transfer: bfloat16 [16384, 256], P('leaf'), may hold values from -0.25 to 0.25
- coupling: bfloat16 [16384, 256], P('leaf'), may hold values from -0.25 to 0.25
Outputs:
- solution: bfloat16 [64, 32768], P(None, 'leaf')
The draws below stay inside these ranges and needn't reach their ends.
All inputs are finite; a program needn't handle non-finite values.
Results may differ from the reference program's by a relative error of at most 0.025.
Values may be sent and summed in bfloat16 or wider, within the bound.
A program may use at most 64 MiB of HBM per device.

```python
import jax
import jax.numpy as jnp
from jax import lax

LEAF = 1024
RANK = 256
COLUMNS = 64
LEVELS = 5
POINTS = 32768
N_LEAF = 32


def shard_levels(stream_key, extent, pieces, low, high):
    def one(axis_at, shards_of):
        heights = jax.random.uniform(jax.random.fold_in(jax.random.fold_in(stream_key, 6), axis_at), (shards_of,), jnp.float32, low / len(pieces), high / len(pieces))
        return jnp.repeat(jnp.exp(heights), extent[axis_at] // shards_of).reshape((-1,) + (1,) * (len(extent) - axis_at - 1))

    loudness = one(*pieces[0])
    for cut in pieces[1:]:
        loudness = loudness * one(*cut)
    return loudness


def noise(rng, dims, scale, reach, shards=(), dtype=jnp.bfloat16):
    level = shard_levels(rng, dims, shards, -0.22, 0.18) if shards else 1.0
    values = jax.random.normal(rng, dims, jnp.float32) * scale * level
    return jnp.minimum(jnp.maximum(values, -reach), reach).astype(dtype)


def setup_inputs(seed: int = 0) -> dict:
    splits = jax.random.split(jax.random.key(seed), 6)
    right_sides = noise(splits[0], (COLUMNS, POINTS), 1.0, 6.0, ((1, 32),))
    leaf_inverse = noise(splits[1], (POINTS, LEAF), LEAF ** -0.5, 0.1875, ((0, 32),))
    leaf_basis = noise(splits[2], (POINTS, RANK), LEAF ** -0.5, 0.1875, ((0, 32),))
    transfer = noise(splits[3], (N_LEAF * 2 * RANK, RANK), (2 * RANK) ** -0.5, 0.25, ((0, 32),))
    coupling = noise(splits[4], (N_LEAF * 2 * RANK, RANK), (2 * RANK) ** -0.5, 0.25, ((0, 32),))
    return dict(right_sides=right_sides, leaf_inverse=leaf_inverse, leaf_basis=leaf_basis, transfer=transfer, coupling=coupling)


def batch_product(left_part, right_part):
    return jnp.einsum("nkr,nrs->nks", left_part.astype(jnp.float32), right_part.astype(jnp.float32), precision=lax.Precision.HIGHEST)


def batch_transposed(left_part, right_part):
    return jnp.einsum("nkr,nsr->nks", left_part.astype(jnp.float32), right_part.astype(jnp.float32), precision=lax.Precision.HIGHEST)


def partner_of(values, distance):
    shaped = values.reshape((-1, 2, distance) + values.shape[1:])
    return shaped[:, ::-1].reshape(values.shape)


def reference(right_sides, leaf_inverse, leaf_basis, transfer, coupling):
    leaves = N_LEAF
    sides = right_sides.reshape(COLUMNS, leaves, LEAF).transpose(1, 0, 2)
    inverses = leaf_inverse.reshape(leaves, LEAF, LEAF)
    bases = leaf_basis.reshape(leaves, LEAF, RANK)
    transfers = transfer.reshape(leaves, 2 * RANK, RANK)
    couplings = coupling.reshape(leaves, 2 * RANK, RANK)
    own_map = transfers[:, :RANK]
    other_map = transfers[:, RANK:]
    from_other = couplings[:, :RANK]
    from_own = couplings[:, RANK:]

    def leaf_skeleton(pair):
        side, basis = pair
        return jnp.dot(side, basis, preferred_element_type=jnp.float32).astype(jnp.bfloat16)

    current = lax.map(leaf_skeleton, (sides, bases))
    own_values = []
    far_values = []
    for tree_level in range(1, LEVELS + 1):
        other = partner_of(current, 2 ** (tree_level - 1))
        own_values.append(current)
        far_values.append(other)
        merged = batch_product(current, own_map) + batch_product(other, other_map)
        current = merged.astype(jnp.bfloat16)
    node_h = current
    for tree_level in range(LEVELS, 0, -1):
        other_h = partner_of(node_h, 2 ** (tree_level - 1))
        total = batch_transposed(node_h, own_map) + batch_transposed(other_h, other_map)
        total = total + batch_product(far_values[tree_level - 1], from_other)
        total = total + batch_product(own_values[tree_level - 1], from_own)
        node_h = total.astype(jnp.bfloat16)

    def leaf_solution(group):
        side, inverse, basis, leaf_h = group
        total = jnp.dot(side, inverse, preferred_element_type=jnp.float32)
        total = total + lax.dot_general(leaf_h, basis, (((1,), (1,)), ((), ())), preferred_element_type=jnp.float32)
        return total.astype(jnp.bfloat16)

    blocks = lax.map(leaf_solution, (sides, inverses, bases, node_h))
    return blocks.transpose(1, 0, 2).reshape(COLUMNS, leaves * LEAF)
```

```python
import functools

import jax
import jax.numpy as jnp
from jax import lax
from jax.experimental import pallas as pl
from jax.experimental.pallas import tpu as pltpu
from jax.sharding import PartitionSpec as P

MESH = pl.DeviceIdType.MESH


def times_matrix(values, matrix):
    return jnp.dot(values, matrix, preferred_element_type=jnp.float32)


def times_transposed(values, matrix):
    return lax.dot_general(
        values, matrix, (((1,), (1,)), ((), ())), preferred_element_type=jnp.float32
    )


def partner_of(me, level):
    bit = 1 << (level - 1)
    return me + bit - 2 * bit * (lax.div(me, bit) % 2)


def kernel(
    levels,
    sides_hbm,
    inverse_hbm,
    basis_hbm,
    transfer_hbm,
    coupling_hbm,
    out_ref,
    sides,
    inverse,
    basis,
    transfer,
    coupling,
    own_t,
    far_t,
    own_h,
    far_h,
    direct,
    near,
    load_sem,
    up_send,
    up_recv,
    down_send,
    down_recv,
):
    me = lax.axis_index("leaf")
    rank = basis.shape[1]
    points = sides.shape[1]
    loads = [
        pltpu.make_async_copy(src, dst, load_sem.at[k])
        for k, (src, dst) in enumerate(
            (
                (sides_hbm, sides),
                (basis_hbm, basis),
                (transfer_hbm, transfer),
                (coupling_hbm, coupling),
                (inverse_hbm, inverse),
            )
        )
    ]
    for load in loads:
        load.start()
    barrier = pltpu.get_barrier_semaphore()
    for level in range(1, levels + 1):
        pl.semaphore_signal(
            barrier, inc=1, device_id=(partner_of(me, level),), device_id_type=MESH
        )

    def exchange(src, dst, send, recv, level):
        copy = pltpu.make_async_remote_copy(
            src_ref=src.at[level - 1],
            dst_ref=dst.at[level - 1],
            send_sem=send.at[level - 1],
            recv_sem=recv.at[level - 1],
            device_id=(partner_of(me, level),),
            device_id_type=MESH,
        )
        copy.start()
        return copy

    loads[0].wait()
    loads[1].wait()
    own_t[0] = times_matrix(sides[...], basis[...]).astype(jnp.bfloat16)
    pl.semaphore_wait(barrier, levels)

    width = points // levels // 128 * 128
    pieces = [(k * width, width) for k in range(levels)]
    pieces[-1] = ((levels - 1) * width, points - (levels - 1) * width)
    copies = []
    for level in range(1, levels + 1):
        copy = exchange(own_t, far_t, up_send, up_recv, level)
        copies.append(copy)
        if level == 1:
            loads[2].wait()
        mine = own_t[level - 1]
        partial = times_matrix(mine, transfer[:rank])
        if level == 2:
            loads[3].wait()
        if level >= 2:
            near[level - 2] = times_matrix(far_t[level - 2], coupling[:rank]) + times_matrix(
                own_t[level - 2], coupling[rank:]
            )
        copy.wait_recv()
        total = partial + times_matrix(far_t[level - 1], transfer[rank:])
        if level < levels:
            own_t[level] = total.astype(jnp.bfloat16)
        else:
            own_h[level - 1] = total.astype(jnp.bfloat16)
    for level in range(levels, 0, -1):
        copy = exchange(own_h, far_h, down_send, down_recv, level)
        copies.append(copy)
        partial = times_transposed(own_h[level - 1], transfer[:rank])
        if level == levels:
            near[level - 1] = times_matrix(far_t[level - 1], coupling[:rank]) + times_matrix(
                own_t[level - 1], coupling[rank:]
            )
            loads[4].wait()
        partial = partial + near[level - 1]
        start, size = pieces[level - 1]
        if size:
            direct[:, start : start + size] = times_matrix(
                sides[...], inverse[:, start : start + size]
            )
        copy.wait_recv()
        total = partial + times_transposed(far_h[level - 1], transfer[rank:])
        if level > 1:
            own_h[level - 2] = total.astype(jnp.bfloat16)
    node_h = total.astype(jnp.bfloat16)
    out_ref[...] = (direct[...] + times_transposed(node_h, basis[...])).astype(jnp.bfloat16)
    for copy in copies:
        copy.wait_send()


def body(right_sides, leaf_inverse, leaf_basis, transfer, coupling):
    levels = lax.axis_size("leaf").bit_length() - 1
    columns = right_sides.shape[0]
    rank = leaf_basis.shape[1]
    steps = pltpu.VMEM((levels, columns, rank), jnp.bfloat16)
    args = (right_sides, leaf_inverse, leaf_basis, transfer, coupling)
    return pl.pallas_call(
        functools.partial(kernel, levels),
        out_shape=jax.ShapeDtypeStruct(right_sides.shape, jnp.bfloat16),
        in_specs=[pl.BlockSpec(memory_space=pl.ANY)] * len(args),
        out_specs=pl.BlockSpec(memory_space=pltpu.VMEM),
        scratch_shapes=[pltpu.VMEM(a.shape, a.dtype) for a in args]
        + [steps] * 4
        + [
            pltpu.VMEM(right_sides.shape, jnp.float32),
            pltpu.VMEM((levels, columns, rank), jnp.float32),
            pltpu.SemaphoreType.DMA((len(args),)),
        ]
        + [pltpu.SemaphoreType.DMA((levels,))] * 4,
        compiler_params=pltpu.CompilerParams(
            collective_id=0, has_side_effects=True, vmem_limit_bytes=32 << 20
        ),
    )(*args)


def solution(mesh):
    placed = (P(None, "leaf"), P("leaf", None), P("leaf", None), P("leaf", None), P("leaf", None))
    return jax.shard_map(
        body, mesh=mesh, in_specs=placed, out_specs=P(None, "leaf"), check_vma=False
    )
```

```python
import functools

import jax
import jax.numpy as jnp
from jax import lax
from jax.experimental import pallas as pl
from jax.experimental.pallas import tpu as pltpu
from jax.sharding import PartitionSpec as P

MESH = pl.DeviceIdType.MESH


def times_matrix(values, matrix):
    return jnp.dot(values, matrix, preferred_element_type=jnp.float32)


def times_transposed(values, matrix):
    return lax.dot_general(
        values, matrix, (((1,), (1,)), ((), ())), preferred_element_type=jnp.float32
    )


def partner_of(me, level):
    bit = 1 << (level - 1)
    return me + bit - 2 * bit * (lax.div(me, bit) % 2)


def kernel(
    levels,
    sides_hbm,
    inverse_hbm,
    basis_hbm,
    transfer_hbm,
    coupling_hbm,
    out_ref,
    sides,
    inverse,
    basis,
    transfer,
    coupling,
    own_t,
    far_t,
    own_h,
    far_h,
    direct,
    near,
    load_sem,
    up_send,
    up_recv,
    down_send,
    down_recv,
):
    me = lax.axis_index("leaf")
    rank = basis.shape[1]
    points = sides.shape[1]
    loads = [
        pltpu.make_async_copy(src, dst, load_sem.at[k])
        for k, (src, dst) in enumerate(
            (
                (sides_hbm, sides),
                (basis_hbm, basis),
                (transfer_hbm, transfer),
                (coupling_hbm, coupling),
                (inverse_hbm, inverse),
            )
        )
    ]
    for load in loads:
        load.start()
    barrier = pltpu.get_barrier_semaphore()
    for level in range(1, levels + 1):
        pl.semaphore_signal(
            barrier, inc=1, device_id=(partner_of(me, level),), device_id_type=MESH
        )

    def exchange(src, dst, send, recv, level):
        copy = pltpu.make_async_remote_copy(
            src_ref=src.at[level - 1],
            dst_ref=dst.at[level - 1],
            send_sem=send.at[level - 1],
            recv_sem=recv.at[level - 1],
            device_id=(partner_of(me, level),),
            device_id_type=MESH,
        )
        copy.start()
        return copy

    loads[0].wait()
    loads[1].wait()
    own_t[0] = times_matrix(sides[...], basis[...]).astype(jnp.bfloat16)
    pl.semaphore_wait(barrier, levels)

    width = points // levels // 128 * 128
    pieces = [(k * width, width) for k in range(levels)]
    pieces[-1] = ((levels - 1) * width, points - (levels - 1) * width)
    copies = []
    for level in range(1, levels + 1):
        copy = exchange(own_t, far_t, up_send, up_recv, level)
        copies.append(copy)
        if level == 1:
            loads[2].wait()
        mine = own_t[level - 1]
        partial = times_matrix(mine, transfer[:rank])
        if level == 2:
            loads[3].wait()
        if level >= 2:
            near[level - 2] = times_matrix(far_t[level - 2], coupling[:rank]) + times_matrix(
                own_t[level - 2], coupling[rank:]
            )
        copy.wait_recv()
        total = partial + times_matrix(far_t[level - 1], transfer[rank:])
        if level < levels:
            own_t[level] = total.astype(jnp.bfloat16)
        else:
            own_h[level - 1] = total.astype(jnp.bfloat16)
    for level in range(levels, 0, -1):
        copy = exchange(own_h, far_h, down_send, down_recv, level)
        copies.append(copy)
        partial = times_transposed(own_h[level - 1], transfer[:rank])
        if level == levels:
            near[level - 1] = times_matrix(far_t[level - 1], coupling[:rank]) + times_matrix(
                own_t[level - 1], coupling[rank:]
            )
            loads[4].wait()
        partial = partial + near[level - 1]
        start, size = pieces[level - 1]
        if size:
            direct[:, start : start + size] = times_matrix(
                sides[...], inverse[:, start : start + size]
            )
        copy.wait_recv()
        total = partial + times_transposed(far_h[level - 1], transfer[rank:])
        if level > 1:
            own_h[level - 2] = total.astype(jnp.bfloat16)
    node_h = total.astype(jnp.bfloat16)
    out_ref[...] = (direct[...] + times_transposed(node_h, basis[...])).astype(jnp.bfloat16)
    for copy in copies:
        copy.wait_send()


def body(right_sides, leaf_inverse, leaf_basis, transfer, coupling):
    levels = lax.axis_size("leaf").bit_length() - 1
    columns = right_sides.shape[0]
    rank = leaf_basis.shape[1]
    steps = pltpu.VMEM((levels, columns, rank), jnp.bfloat16)
    args = (right_sides, leaf_inverse, leaf_basis, transfer, coupling)
    return pl.pallas_call(
        functools.partial(kernel, levels),
        out_shape=jax.ShapeDtypeStruct(right_sides.shape, jnp.bfloat16),
        in_specs=[pl.BlockSpec(memory_space=pl.ANY)] * len(args),
        out_specs=pl.BlockSpec(memory_space=pltpu.VMEM),
        scratch_shapes=[pltpu.VMEM(a.shape, a.dtype) for a in args]
        + [steps] * 4
        + [
            pltpu.VMEM(right_sides.shape, jnp.float32),
            pltpu.VMEM((levels, columns, rank), jnp.float32),
            pltpu.SemaphoreType.DMA((len(args),)),
        ]
        + [pltpu.SemaphoreType.DMA((levels,))] * 4,
        compiler_params=pltpu.CompilerParams(
            collective_id=0, has_side_effects=True, vmem_limit_bytes=60 << 20
        ),
    )(*args)


def solution(mesh):
    placed = (P(None, "leaf"), P("leaf", None), P("leaf", None), P("leaf", None), P("leaf", None))
    return jax.shard_map(
        body, mesh=mesh, in_specs=placed, out_specs=P(None, "leaf"), check_vma=False
    )
```

```python
import functools

import jax
import jax.numpy as jnp
from jax import lax
from jax.experimental import pallas as pl
from jax.experimental.pallas import tpu as pltpu
from jax.sharding import PartitionSpec as P

MESH = pl.DeviceIdType.MESH


def times_matrix(values, matrix):
    return jnp.dot(values, matrix, preferred_element_type=jnp.float32)


def times_transposed(values, matrix):
    return lax.dot_general(
        values, matrix, (((1,), (1,)), ((), ())), preferred_element_type=jnp.float32
    )


def rounded(values):
    return values.astype(jnp.bfloat16)


def flipped(me, levels):
    for level in levels:
        bit = 1 << (level - 1)
        me = me + bit - 2 * bit * (lax.div(me, bit) % 2)
    return me


def rounds(levels):
    up = [(level,) for level in range(1, min(levels, 2) + 1)]
    up += [(low, low + 1) if low < levels else (low,) for low in range(3, levels + 1, 2)]
    return up, [(level,) for level in range(levels, 0, -1)]


def count_messages(up, down):
    return sum(3 if len(r) == 2 else 1 for r in up) + sum(4 if len(r) == 2 else 1 for r in down)


def kernel(
    levels,
    sides_hbm,
    inverse_hbm,
    basis_hbm,
    transfer_hbm,
    coupling_hbm,
    out_ref,
    sides,
    inverse,
    basis,
    transfer,
    coupling,
    maps,
    turned,
    own_t,
    far_t,
    own_h,
    near,
    near_out,
    inbox,
    direct,
    load_sem,
    send_sem,
    recv_sem,
    maps_send,
    maps_recv,
):
    me = lax.axis_index("leaf")
    rank = basis.shape[1]
    up, down = rounds(levels)
    loads = [
        pltpu.make_async_copy(src, dst, load_sem.at[k])
        for k, (src, dst) in enumerate(
            (
                (sides_hbm, sides),
                (basis_hbm, basis),
                (transfer_hbm, transfer),
                (coupling_hbm, coupling),
                (inverse_hbm, inverse),
            )
        )
    ]
    for load in loads:
        load.start()
    peers = sorted({(level,) for level in range(1, levels + 1)} | {
        tuple(sorted(r)) for r in up + down if len(r) == 2
    })
    barrier = pltpu.get_barrier_semaphore()
    for peer in peers:
        pl.semaphore_signal(barrier, inc=1, device_id=(flipped(me, peer),), device_id_type=MESH)

    sent = []
    slots = iter(range(count_messages(up, down)))

    def post(src, peer):
        slot = next(slots)
        copy = pltpu.make_async_remote_copy(
            src_ref=src,
            dst_ref=inbox.at[slot],
            send_sem=send_sem.at[slot],
            recv_sem=recv_sem.at[slot],
            device_id=(flipped(me, peer),),
            device_id_type=MESH,
        )
        copy.start()
        sent.append(copy)
        return copy, inbox.at[slot]

    def take(message):
        message[0].wait_recv()
        return message[1][...]

    maps_copy = {}

    def post_maps(level):
        index = level // 2 - 1
        copy = pltpu.make_async_remote_copy(
            src_ref=transfer,
            dst_ref=maps.at[index],
            send_sem=maps_send.at[index],
            recv_sem=maps_recv.at[index],
            device_id=(flipped(me, (level,)),),
            device_id_type=MESH,
        )
        copy.start()
        sent.append(copy)
        maps_copy[level] = [copy, False]

    def maps_of(level):
        entry = maps_copy[level]
        if not entry[1]:
            entry[0].wait_recv()
            entry[1] = True
        return maps.at[level // 2 - 1]

    loads[0].wait()
    loads[1].wait()
    own_t[0] = rounded(times_matrix(sides[...], basis[...]))
    loads[2].wait()
    pl.semaphore_wait(barrier, len(peers))

    near_in = {}
    later = []

    def idle():
        while later:
            later.pop(0)()

    def add_near(level):
        def run():
            near[level - 1] = times_matrix(far_t[level - 1], coupling[:rank]) + times_matrix(
                own_t[level - 1], coupling[rank:]
            )
            for high, *low in down:
                if low and high == level:
                    near_out[level - 1] = rounded(near[level - 1])
                    near_in[level] = post(near_out.at[level - 1], tuple(low))

        later.append(run)

    def keep(level, values):
        if level < levels:
            own_t[level] = values
        else:
            own_h[levels - 1] = values

    def turn(index, source):
        for half in (slice(0, rank), slice(rank, 2 * rank)):
            turned[index, half] = source[half].T

    def add_direct():
        loads[4].wait()
        direct[...] = times_matrix(sides[...], inverse[...])

    for group in up:
        low, high = group[0], group[-1]
        mine = own_t.at[low - 1]
        if len(group) == 2:
            both = post(mine, group)
        first = post(mine, (low,))
        if len(group) == 2:
            second = post(mine, (high,))
        if low == 1:
            for level in range(4, levels + 1, 2):
                post_maps(level)
            loads[3].wait()
        if low == 2:
            later.append(lambda: turn(0, transfer))
            later.append(add_direct)
        partial = times_matrix(mine[...], transfer[:rank])
        idle()
        far_t[low - 1] = take(first)
        total = rounded(partial + times_matrix(far_t[low - 1], transfer[rank:]))
        keep(low, total)
        add_near(low)
        if len(group) == 2:
            theirs = maps_of(high)
            partial = times_matrix(total, transfer[:rank])
            other = times_matrix(take(second), theirs[:rank])
            other = rounded(other + times_matrix(take(both), theirs[rank:]))
            far_t[high - 1] = other
            keep(high, rounded(partial + times_matrix(other, transfer[rank:])))
            add_near(high)

    for group in down:
        high, low = group[0], group[-1]
        mine = own_h.at[high - 1]
        if len(group) == 2:
            both = post(mine, group)
        first = post(mine, (high,))
        if len(group) == 2:
            second = post(mine, (low,))
        partial = times_matrix(mine[...], turned[0, :rank])
        idle()
        partial = partial + near[high - 1]
        if len(group) == 2:
            other = times_matrix(take(second), turned[low // 2, :rank])
            other = other + take(near_in[high]).astype(jnp.float32)
        total = rounded(
            partial + times_matrix(take(first), turned[0, rank:])
        )
        if len(group) == 2:
            partial = times_matrix(total, turned[0, :rank]) + near[low - 1]
            other = rounded(other + times_matrix(take(both), turned[low // 2, rank:]))
            total = rounded(partial + times_matrix(other, turned[0, rank:]))
        if low > 1:
            own_h[low - 2] = total
    if levels < 2:
        add_direct()
    out_ref[...] = rounded(direct[...] + times_transposed(total, basis[...]))
    for copy in sent:
        copy.wait_send()


def body(right_sides, leaf_inverse, leaf_basis, transfer, coupling):
    levels = lax.axis_size("leaf").bit_length() - 1
    columns = right_sides.shape[0]
    rank = leaf_basis.shape[1]
    messages = count_messages(*rounds(levels))
    shared = max(levels // 2, 1)
    steps = pltpu.VMEM((levels, columns, rank), jnp.bfloat16)
    args = (right_sides, leaf_inverse, leaf_basis, transfer, coupling)
    return pl.pallas_call(
        functools.partial(kernel, levels),
        out_shape=jax.ShapeDtypeStruct(right_sides.shape, jnp.bfloat16),
        in_specs=[pl.BlockSpec(memory_space=pl.ANY)] * len(args),
        out_specs=pl.BlockSpec(memory_space=pltpu.VMEM),
        scratch_shapes=[pltpu.VMEM(a.shape, a.dtype) for a in args]
        + [pltpu.VMEM((shared,) + transfer.shape, jnp.bfloat16)]
        + [pltpu.VMEM((shared + 1,) + transfer.shape, jnp.bfloat16)]
        + [steps] * 3
        + [
            pltpu.VMEM((levels, columns, rank), jnp.float32),
            steps,
            pltpu.VMEM((messages, columns, rank), jnp.bfloat16),
            pltpu.VMEM(right_sides.shape, jnp.float32),
            pltpu.SemaphoreType.DMA((len(args),)),
            pltpu.SemaphoreType.DMA((messages,)),
            pltpu.SemaphoreType.DMA((messages,)),
            pltpu.SemaphoreType.DMA((shared,)),
            pltpu.SemaphoreType.DMA((shared,)),
        ],
        compiler_params=pltpu.CompilerParams(
            collective_id=0, has_side_effects=True, vmem_limit_bytes=60 << 20
        ),
    )(*args)


def solution(mesh):
    placed = (P(None, "leaf"), P("leaf", None), P("leaf", None), P("leaf", None), P("leaf", None))
    return jax.shard_map(
        body, mesh=mesh, in_specs=placed, out_specs=P(None, "leaf"), check_vma=False
    )
```

```python
import functools

import jax
import jax.numpy as jnp
from jax import lax
from jax.experimental import pallas as pl
from jax.experimental.pallas import tpu as pltpu
from jax.sharding import PartitionSpec as P

MESH = pl.DeviceIdType.MESH


def times_matrix(values, matrix):
    return jnp.dot(values, matrix, preferred_element_type=jnp.float32)


def times_transposed(values, matrix):
    return lax.dot_general(
        values, matrix, (((1,), (1,)), ((), ())), preferred_element_type=jnp.float32
    )


def rounded(values):
    return values.astype(jnp.bfloat16)


def flipped(me, levels):
    for level in levels:
        bit = 1 << (level - 1)
        me = me + bit - 2 * bit * (lax.div(me, bit) % 2)
    return me


def rounds(levels):
    up = [(level,) for level in range(1, min(levels, 2) + 1)]
    up += [(low, low + 1) if low < levels else (low,) for low in range(3, levels + 1, 2)]
    return up, [(level,) for level in range(levels, 0, -1)]


def count_messages(up, down):
    return sum(3 if len(r) == 2 else 1 for r in up) + sum(4 if len(r) == 2 else 1 for r in down)


def kernel(
    levels,
    sides_hbm,
    inverse_hbm,
    basis_hbm,
    transfer_hbm,
    coupling_hbm,
    out_ref,
    sides,
    inverse,
    basis,
    transfer,
    coupling,
    maps,
    turned,
    own_t,
    far_t,
    own_h,
    near,
    near_out,
    inbox,
    direct,
    load_sem,
    send_sem,
    recv_sem,
    maps_send,
    maps_recv,
):
    me = lax.axis_index("leaf")
    rank = basis.shape[1]
    up, down = rounds(levels)
    loads = [
        pltpu.make_async_copy(src, dst, load_sem.at[k])
        for k, (src, dst) in enumerate(
            (
                (sides_hbm, sides),
                (basis_hbm, basis),
                (transfer_hbm, transfer),
                (coupling_hbm, coupling),
                (inverse_hbm, inverse),
            )
        )
    ]
    for load in loads:
        load.start()
    peers = sorted({(level,) for level in range(1, levels + 1)} | {
        tuple(sorted(r)) for r in up + down if len(r) == 2
    })
    barrier = pltpu.get_barrier_semaphore()
    for peer in peers:
        pl.semaphore_signal(barrier, inc=1, device_id=(flipped(me, peer),), device_id_type=MESH)

    sent = []
    slots = iter(range(count_messages(up, down)))

    def post(src, peer):
        slot = next(slots)
        copy = pltpu.make_async_remote_copy(
            src_ref=src,
            dst_ref=inbox.at[slot],
            send_sem=send_sem.at[slot],
            recv_sem=recv_sem.at[slot],
            device_id=(flipped(me, peer),),
            device_id_type=MESH,
        )
        copy.start()
        sent.append(copy)
        return copy, inbox.at[slot]

    def take(message):
        message[0].wait_recv()
        return message[1][...]

    maps_copy = {}

    def post_maps(level):
        index = level // 2 - 1
        copies = []
        for half in range(2):
            rows = pl.ds(half * rank, rank)
            copy = pltpu.make_async_remote_copy(
                src_ref=transfer.at[rows],
                dst_ref=maps.at[index, rows],
                send_sem=maps_send.at[index, half],
                recv_sem=maps_recv.at[index, half],
                device_id=(flipped(me, (level,)),),
                device_id_type=MESH,
            )
            copy.start()
            copies.append(copy)
            sent.append(copy)
        maps_copy[level] = [copies, False]

    def maps_of(level):
        entry = maps_copy[level]
        if not entry[1]:
            for copy in entry[0]:
                copy.wait_recv()
            entry[1] = True
        return maps.at[level // 2 - 1]

    loads[0].wait()
    loads[1].wait()
    own_t[0] = rounded(times_matrix(sides[...], basis[...]))
    loads[2].wait()
    pl.semaphore_wait(barrier, len(peers))

    near_in = {}
    later = []

    def idle():
        while later:
            later.pop(0)()

    def add_near(level):
        def run():
            near[level - 1] = times_matrix(far_t[level - 1], coupling[:rank]) + times_matrix(
                own_t[level - 1], coupling[rank:]
            )
            for high, *low in down:
                if low and high == level:
                    near_out[level - 1] = rounded(near[level - 1])
                    near_in[level] = post(near_out.at[level - 1], tuple(low))

        later.append(run)

    def keep(level, values):
        if level < levels:
            own_t[level] = values
        else:
            own_h[levels - 1] = values

    def turn(index, source):
        for half in (slice(0, rank), slice(rank, 2 * rank)):
            turned[index, half] = source[half].T

    def add_direct():
        loads[4].wait()
        direct[...] = times_matrix(sides[...], inverse[...])

    for group in up:
        low, high = group[0], group[-1]
        mine = own_t.at[low - 1]
        if len(group) == 2:
            both = post(mine, group)
        first = post(mine, (low,))
        if len(group) == 2:
            second = post(mine, (high,))
        if low == 1:
            for level in range(4, levels + 1, 2):
                post_maps(level)
            loads[3].wait()
        if low == 2:
            later.append(lambda: turn(0, transfer))
            later.append(add_direct)
        partial = times_matrix(mine[...], transfer[:rank])
        idle()
        far_t[low - 1] = take(first)
        total = rounded(partial + times_matrix(far_t[low - 1], transfer[rank:]))
        keep(low, total)
        add_near(low)
        if len(group) == 2:
            theirs = maps_of(high)
            partial = times_matrix(total, transfer[:rank])
            other = times_matrix(take(second), theirs[:rank])
            other = rounded(other + times_matrix(take(both), theirs[rank:]))
            far_t[high - 1] = other
            keep(high, rounded(partial + times_matrix(other, transfer[rank:])))
            add_near(high)

    for group in down:
        high, low = group[0], group[-1]
        mine = own_h.at[high - 1]
        if len(group) == 2:
            both = post(mine, group)
        first = post(mine, (high,))
        if len(group) == 2:
            second = post(mine, (low,))
        partial = times_matrix(mine[...], turned[0, :rank])
        idle()
        partial = partial + near[high - 1]
        if len(group) == 2:
            other = times_matrix(take(second), turned[low // 2, :rank])
            other = other + take(near_in[high]).astype(jnp.float32)
        total = rounded(
            partial + times_matrix(take(first), turned[0, rank:])
        )
        if len(group) == 2:
            partial = times_matrix(total, turned[0, :rank]) + near[low - 1]
            other = rounded(other + times_matrix(take(both), turned[low // 2, rank:]))
            total = rounded(partial + times_matrix(other, turned[0, rank:]))
        if low > 1:
            own_h[low - 2] = total
    if levels < 2:
        add_direct()
    out_ref[...] = rounded(direct[...] + times_transposed(total, basis[...]))
    for copy in sent:
        copy.wait_send()


def body(right_sides, leaf_inverse, leaf_basis, transfer, coupling):
    levels = lax.axis_size("leaf").bit_length() - 1
    columns = right_sides.shape[0]
    rank = leaf_basis.shape[1]
    messages = count_messages(*rounds(levels))
    shared = max(levels // 2, 1)
    steps = pltpu.VMEM((levels, columns, rank), jnp.bfloat16)
    args = (right_sides, leaf_inverse, leaf_basis, transfer, coupling)
    return pl.pallas_call(
        functools.partial(kernel, levels),
        out_shape=jax.ShapeDtypeStruct(right_sides.shape, jnp.bfloat16),
        in_specs=[pl.BlockSpec(memory_space=pl.ANY)] * len(args),
        out_specs=pl.BlockSpec(memory_space=pltpu.VMEM),
        scratch_shapes=[pltpu.VMEM(a.shape, a.dtype) for a in args]
        + [pltpu.VMEM((shared,) + transfer.shape, jnp.bfloat16)]
        + [pltpu.VMEM((shared + 1,) + transfer.shape, jnp.bfloat16)]
        + [steps] * 3
        + [
            pltpu.VMEM((levels, columns, rank), jnp.float32),
            steps,
            pltpu.VMEM((messages, columns, rank), jnp.bfloat16),
            pltpu.VMEM(right_sides.shape, jnp.float32),
            pltpu.SemaphoreType.DMA((len(args),)),
            pltpu.SemaphoreType.DMA((messages,)),
            pltpu.SemaphoreType.DMA((messages,)),
            pltpu.SemaphoreType.DMA((shared, 2)),
            pltpu.SemaphoreType.DMA((shared, 2)),
        ],
        compiler_params=pltpu.CompilerParams(
            collective_id=0, has_side_effects=True, vmem_limit_bytes=60 << 20
        ),
    )(*args)


def solution(mesh):
    placed = (P(None, "leaf"), P("leaf", None), P("leaf", None), P("leaf", None), P("leaf", None))
    return jax.shard_map(
        body, mesh=mesh, in_specs=placed, out_specs=P(None, "leaf"), check_vma=False
    )
```
